512 devices in a mesh: dp: 64 (over z_hi, y, x), tensor: 8 (over z_lo, core).
Axes of the slice: x: 4, y: 8, z: 8 (z_hi: 2, z_lo: 4; z = z_hi * 4 + z_lo), core: 2. Of those that a mesh axis runs over, the one named last changes fastest.
Arguments:
- inputs: bfloat16 [131072, 1408], P('dp'), may hold values from -6 to 6
- up_weight: bfloat16 [1408, 6144], P(None, 'tensor'), may hold values from -0.15625 to 0.15625
- out_grad: bfloat16 [131072, 1408], P('dp', 'tensor'), may hold values from -6 to 6
- proj_in: bfloat16 [6144, 64], P('tensor'), may hold values from -0.078125 to 0.078125
- proj_out: bfloat16 [1408, 64], P('tensor'), may hold values from -0.15625 to 0.15625
- queries: bfloat16 [1024, 4096], P('dp', 'tensor'), may hold values from -0.009765625 to 0.009765625
- lengths: int32 [64, 8], P('dp'), may hold values from 1 to 3, 16 in all within a row
Outputs:
- scores: float32 [512, 1024], P('dp', 'tensor')
The draws below stay inside these ranges and needn't reach their ends.
Inputs may be any that keep to these rules, and one draw needn't show every extreme that they name: Each row of lengths sums to 16, and some scene of each row has 3 blocks.
All inputs are finite; a program needn't handle non-finite values.
Results may differ from the reference program's by a relative error of at most 0.014.
Values may be sent and summed in bfloat16 or wider, within the bound.
No kernel may reach another device: no remote copies, remote signals or barrier semaphores. Data moves between devices by JAX's collectives and lax.ppermute only.
A program may use at most 64 MiB of HBM per device.

```python
import math
import jax
import jax.numpy as jnp
import numpy as np
from jax import lax

D = 1408
FF = 6144
RANK = 64
QUERIES = 1024
BLOCK = 128
MOST = 3
TOK_DEV = 2048
SCENES_DEV = 8
FEAT = 4096
TOKENS = 131072
SCENES = 512
N_DP = 64


def steps_of(own_key, dims, pieces, low, top_value):
    level = 1.0
    for dim, blocks in pieces:
        heights = jax.random.uniform(jax.random.fold_in(jax.random.fold_in(own_key, 6), dim), (blocks,), jnp.float32, low / len(pieces), top_value / len(pieces))
        level = level * jnp.repeat(jnp.exp(heights), dims[dim] // blocks).reshape((-1,) + (1,) * (len(dims) - 1 - dim))
    return level


def length_profile(count, total, limit, skew):
    weights = [(1 << 20) // math.isqrt(grade ** skew) + 1 for grade in range(2, count + 1)]
    surplus, counts = total - limit - (count - 1), [1] * (count - 1)
    while surplus > 0:
        candidates = [i for i in range(count - 1) if counts[i] < limit]
        pool, remaining = sum([weights[i] for i in candidates]), surplus
        for i in candidates:
            more = min(limit - counts[i], max(1, remaining * weights[i] // pool), surplus)
            counts[i] = counts[i] + more
            surplus = surplus - more
    return np.array([limit] + counts)


def uneven_parts(key, number_of, total, limit, skew):
    if number_of == 2:
        one = jax.random.randint(key, (), max(1, total - limit), min(limit, total - 1) + 1)
        return jnp.stack([one, total - one])
    tallies = jnp.asarray(length_profile(number_of, total, limit, skew), jnp.int32)
    pairs = (number_of - 1) // 2
    giver, taker = tallies[1:1 + 2 * pairs:2], tallies[2:2 + 2 * pairs:2]
    slack = jnp.minimum(giver - 1, limit - taker)
    passed = jax.random.randint(jax.random.fold_in(key, 1), (pairs,), 0, 1 << 20) % (slack + 1)
    tallies = tallies.at[1:1 + 2 * pairs:2].set(giver - passed).at[2:2 + 2 * pairs:2].set(taker + passed)
    return tallies[jax.random.permutation(jax.random.fold_in(key, 2), number_of)]


def noise(rng, shape, spread, reach, cuts=(), held_as=jnp.bfloat16):
    level = steps_of(rng, shape, cuts, -0.22, 0.18) if cuts else 1.0
    values = jax.random.normal(rng, shape, jnp.float32) * spread * level
    return jnp.minimum(jnp.maximum(values, -reach), reach).astype(held_as)


def setup_inputs(seed: int = 0) -> dict:
    seeds = jax.random.split(jax.random.key(seed), 8)
    return {
        "inputs": noise(seeds[0], (TOKENS, D), 1.0, 6.0, ((0, 64),)),
        "up_weight": noise(seeds[1], (D, FF), D ** -0.5, 0.15625, ((1, 8),)),
        "out_grad": noise(seeds[2], (TOKENS, D), 1.0, 6.0, ((0, 64), (1, 8))),
        "proj_in": noise(seeds[3], (FF, RANK), FF ** -0.5, 0.078125, ((0, 8),)),
        "proj_out": noise(seeds[4], (D, RANK), D ** -0.5, 0.15625, ((0, 8),)),
        "queries": noise(seeds[5], (QUERIES, FEAT), (FEAT * 100) ** -0.5, 0.009765625, ((0, 64), (1, 8))),
        "lengths": jax.vmap(lambda own: uneven_parts(own, SCENES_DEV, TOK_DEV // 128, MOST, 2))(jax.random.split(seeds[6], N_DP)).reshape((N_DP, SCENES_DEV)).astype(jnp.int32),
    }


def group_features(args):
    inputs, out_grad, lengths, up_weight, proj_in, proj_out = args
    hidden = jax.nn.gelu(jnp.dot(inputs, up_weight, preferred_element_type=jnp.float32), approximate=False).astype(jnp.bfloat16)
    in_proj = jnp.dot(hidden, proj_in, preferred_element_type=jnp.float32)
    out_proj = jnp.dot(out_grad, proj_out, preferred_element_type=jnp.float32)
    ends = BLOCK * jnp.cumsum(lengths).astype(jnp.int32)
    starts = ends - BLOCK * lengths
    position = jnp.arange(TOK_DEV, dtype=jnp.int32)
    member = ((position[None, :] >= starts[:, None]) & (position[None, :] < ends[:, None])).astype(jnp.float32)
    feats = jnp.einsum("st,ti,tj->sij", member, out_proj, in_proj)
    return feats.reshape(SCENES_DEV, FEAT)


def reference(inputs, up_weight, out_grad, proj_in, proj_out, queries, lengths):
    inputs_groups = inputs.reshape(N_DP, TOK_DEV, D)
    grad_groups = out_grad.reshape(N_DP, TOK_DEV, D)
    feats = lax.map(lambda item: group_features((item[0], item[1], item[2], up_weight, proj_in, proj_out)), (inputs_groups, grad_groups, lengths))
    features = feats.reshape(SCENES, FEAT).astype(jnp.bfloat16)
    return lax.dot_general(features, queries, (((1,), (1,)), ((), ())), preferred_element_type=jnp.float32)
```

```python
import jax
import jax.numpy as jnp
from jax import lax
from jax.experimental import pallas as pl
from jax.experimental.pallas import tpu as pltpu
from jax.sharding import Mesh
from jax.sharding import PartitionSpec as P

bf16 = jnp.bfloat16
f32 = jnp.float32

PARTS = ("z", "y2", "y1", "y0", "x1", "x0", "zl", "c")
SIZES = (2, 2, 2, 2, 2, 2, 4, 2)
DP = PARTS[:6]
TENSOR = PARTS[6:]
SWAP = [(0, 1), (1, 0)]
ORDER = ("x0", "y0", "x1", "y1", "y2", "z")
VMEM = pl.BlockSpec(memory_space=pltpu.VMEM)
ANY = pl.BlockSpec(memory_space=pl.ANY)
SMEM = pl.BlockSpec(memory_space=pltpu.SMEM)

ERF = (
    7.97884332e-01,
    3.63339859e-02,
    -3.29015638e-05,
    -5.53135740e-05,
    3.98006372e-06,
    -1.34189628e-07,
    1.82394749e-09,
)


def gelu(x):
    u = x * x
    g = ERF[-1]
    for coef in ERF[-2::-1]:
        g = g * u + coef
    half = 0.5 * x
    return half + half * jnp.tanh(x * g)


def near(x):
    return pltpu.with_memory_space_constraint(x, pltpu.VMEM)


def scene_kernel(len_ref, out_ref):
    ends, end = [], 0
    for s in range(8):
        end = end + len_ref[0, s]
        ends.append(end)
    for block in range(16):
        scene = 0
        for s in range(7):
            scene = scene + (block >= ends[s]).astype(jnp.int32)
        out_ref[block] = scene


def scene_of_block(lengths):
    return pl.pallas_call(
        scene_kernel,
        in_specs=[SMEM],
        out_specs=SMEM,
        out_shape=jax.ShapeDtypeStruct((16,), jnp.int32),
        compiler_params=pltpu.CompilerParams(vmem_limit_bytes=2**20),
        cost_estimate=pl.CostEstimate(flops=20 * 10**9, bytes_accessed=64, transcendentals=0),
    )(lengths)


def in_kernel(x_ref, w_ref, p_ref, o_ref):
    width = 256
    x = x_ref[...]
    total = None
    for n in range(w_ref.shape[1] // width):
        part = slice(n * width, (n + 1) * width)
        z = lax.dot_general(
            w_ref[:, part], x, (((0,), (1,)), ((), ())), preferred_element_type=f32
        )
        term = jnp.dot(p_ref[:, part], gelu(z).astype(bf16), preferred_element_type=f32)
        total = term if total is None else total + term
    half = x.shape[0] // 2
    o_ref[0] = total[:, :half].astype(bf16)
    o_ref[1] = total[:, half:].astype(bf16)


def in_project(x, w, p):
    rows, width = x.shape
    hidden = w.shape[1]
    return pl.pallas_call(
        in_kernel,
        in_specs=[VMEM] * 3,
        out_specs=VMEM,
        out_shape=jax.ShapeDtypeStruct((2, p.shape[0], rows // 2), bf16),
        compiler_params=pltpu.CompilerParams(vmem_limit_bytes=32 * 2**20),
        cost_estimate=pl.CostEstimate(
            flops=2 * rows * hidden * (width + 256),
            bytes_accessed=2 * (rows * width + width * hidden),
            transcendentals=rows * hidden,
        ),
    )(near(x), near(w), near(p))


def feature_kernel(scene_ref, o1_ref, o2_ref, i_ref, out_ref, acc):
    core = lax.axis_index("c")
    acc[...] = jnp.zeros(acc.shape, f32)
    for turn, o_ref in enumerate((o1_ref, o2_ref)):
        half = core ^ turn
        for k in range(8):
            cols = slice(k * 128, (k + 1) * 128)
            acc[scene_ref[half * 8 + k]] += lax.dot_general(
                o_ref[:, cols],
                i_ref[half, :, cols],
                (((1,), (1,)), ((), ())),
                preferred_element_type=f32,
            )
    for m in range(4):
        pair = jnp.concatenate([acc[m], acc[m + 4]], axis=1).astype(bf16)
        for t in range(8):
            out_ref[t, 8 * m : 8 * m + 8, :] = pair[8 * t : 8 * t + 8, :]


def features(scene, o1, o2, i):
    return pl.pallas_call(
        feature_kernel,
        in_specs=[SMEM, VMEM, VMEM, VMEM],
        out_specs=VMEM,
        out_shape=jax.ShapeDtypeStruct((8, 32, 128), bf16),
        scratch_shapes=[pltpu.VMEM((8, 64, 64), f32)],
        compiler_params=pltpu.CompilerParams(vmem_limit_bytes=8 * 2**20),
        cost_estimate=pl.CostEstimate(flops=20 * 10**9, bytes_accessed=2**20, transcendentals=0),
    )(scene, near(o1), near(o2), near(i))


def score_kernel(f_ref, q1_ref, q2_ref, out_ref, own, turned, feat):
    group = lax.axis_index("z") * 4 + lax.axis_index("y2") * 2
    total = f_ref[0].astype(f32)
    for t in range(1, 8):
        total = total + f_ref[t].astype(f32)
    own[...] = total
    turned[...] = pltpu.roll(total, 64, 1)
    low = lax.broadcasted_iota(jnp.int32, (4, 128), 1) < 64
    for p in range(4):
        even, odd = pl.ds(2 * p, 4, stride=8), pl.ds(2 * p + 1, 4, stride=8)
        cols = slice(128 * p, 128 * p + 128)
        feat[0:4, cols] = jnp.where(low, own[even, :], turned[odd, :])
        feat[4:8, cols] = jnp.where(low, turned[even, :], own[odd, :])
    f = feat[...].astype(bf16)
    lanes = lax.broadcasted_iota(jnp.int32, (8, 128), 1)
    for t in range(8):
        rows = []
        for b in range(8):
            bits = dict(z=t & 4, y2=t & 2, y1=t & 1, y0=b & 4, x1=b & 2, x0=b & 1)
            row = 0
            for axis in ORDER:
                row = 2 * row + (bits[axis] > 0)
            ref, row = (q1_ref, row) if row < 32 else (q2_ref, row - 32)
            rows.append(ref[16 * row : 16 * row + 16, :])
        x = lax.dot_general(
            f, jnp.concatenate(rows, axis=0), (((1,), (1,)), ((), ())), preferred_element_type=f32
        )
        for axis, width in (("y0", 64), ("x0", 16)):
            other = jnp.where((lanes & width) == 0, pltpu.roll(x, 128 - width, 1), pltpu.roll(x, width, 1))
            x = jnp.where(lax.axis_index(axis) == 1, other, x)
        out_ref[t ^ group] = x


def partial_scores(f, q1, q2):
    return pl.pallas_call(
        score_kernel,
        in_specs=[VMEM] * 3,
        out_specs=VMEM,
        out_shape=jax.ShapeDtypeStruct((8, 8, 128), f32),
        scratch_shapes=[
            pltpu.VMEM((32, 128), f32),
            pltpu.VMEM((32, 128), f32),
            pltpu.VMEM((8, 512), f32),
        ],
        compiler_params=pltpu.CompilerParams(vmem_limit_bytes=8 * 2**20),
        cost_estimate=pl.CostEstimate(flops=2 * 256 * 512 * 1024, bytes_accessed=2**20, transcendentals=0),
    )(f, q1, q2)


def gather(x, axes):
    count = 2 ** len(axes)
    x = lax.all_to_all(jnp.broadcast_to(x[None], (count,) + x.shape), axes, 0, 0)
    return x.reshape((-1,) + x.shape[2:])


NEAR = [(0, 1), (1, 0), (2, 3), (3, 2)]
FAR = [(0, 2), (2, 0), (1, 3), (3, 1)]
tie = lax.optimization_barrier


def local(inputs, up_weight, out_grad, proj_in, proj_out, queries, lengths):
    core = lax.axis_index("c")
    scene, p = tie((scene_of_block(lengths), proj_in.T))
    q = jnp.concatenate([queries, lax.ppermute(queries, "z", SWAP)], axis=0)
    o = lax.dot_general(proj_out, out_grad, (((0,), (1,)), ((), ())), preferred_element_type=f32)
    half = o.shape[1] // 2
    o1 = lax.dynamic_slice_in_dim(o, core * half, half, 1)
    o2 = lax.dynamic_slice_in_dim(o, (1 - core) * half, half, 1)
    o = o1 + lax.ppermute(o2.astype(bf16), "c", SWAP).astype(f32)
    i = in_project(inputs, up_weight, p)

    o, q, i = tie((o, q, i))
    o = o + lax.ppermute(o.astype(bf16), "zl", NEAR).astype(f32)
    o = o + lax.ppermute(o.astype(bf16), "zl", FAR).astype(f32)
    o1 = o.astype(bf16)
    o2 = lax.ppermute(o1, "c", SWAP)
    q = jnp.concatenate([q, lax.ppermute(q, "y2", SWAP)], axis=0)
    q = gather(q, ("x1", "y1"))
    q, o1, o2 = tie((q, o1, o2))
    q = jnp.concatenate([q, lax.ppermute(q, "y0", SWAP)], axis=0)
    f = features(scene, o1, o2, i)
    q, f = tie((q, f))
    q2 = lax.ppermute(q, "x0", SWAP)
    f = lax.all_to_all(f, TENSOR, 0, 0)
    scores = partial_scores(near(f), near(q), near(q2))
    return jnp.sum(lax.all_to_all(scores, TENSOR, 0, 0), axis=0)


def solution(mesh):
    fine = Mesh(mesh.devices.reshape(SIZES), PARTS)
    return jax.shard_map(
        local,
        mesh=fine,
        in_specs=(
            P(DP, None),
            P(None, TENSOR),
            P(DP, TENSOR),
            P(TENSOR, None),
            P(TENSOR, None),
            P(DP, TENSOR),
            P(DP, None),
        ),
        out_specs=P(DP, TENSOR),
        check_vma=False,
    )
```

```python
import jax
import jax.numpy as jnp
from jax import lax
from jax.experimental import pallas as pl
from jax.experimental.pallas import tpu as pltpu
from jax.sharding import Mesh
from jax.sharding import PartitionSpec as P

bf16 = jnp.bfloat16
f32 = jnp.float32

PARTS = ("z", "y2", "y1", "y0", "x1", "x0", "zl", "c")
SIZES = (2, 2, 2, 2, 2, 2, 4, 2)
DP = PARTS[:6]
TENSOR = PARTS[6:]
SWAP = [(0, 1), (1, 0)]
ORDER = ("y0", "x0", "y1", "x1", "y2", "z")
VMEM = pl.BlockSpec(memory_space=pltpu.VMEM)
ANY = pl.BlockSpec(memory_space=pl.ANY)
SMEM = pl.BlockSpec(memory_space=pltpu.SMEM)

ERF = (
    7.97884332e-01,
    3.63339859e-02,
    -3.29015638e-05,
    -5.53135740e-05,
    3.98006372e-06,
    -1.34189628e-07,
    1.82394749e-09,
)


def gelu(x):
    u = x * x
    g = ERF[-1]
    for coef in ERF[-2::-1]:
        g = g * u + coef
    half = 0.5 * x
    return half + half * jnp.tanh(x * g)


def near(x):
    return pltpu.with_memory_space_constraint(x, pltpu.VMEM)


def scene_kernel(len_ref, out_ref):
    ends, end = [], 0
    for s in range(8):
        end = end + len_ref[0, s]
        ends.append(end)
    for block in range(16):
        scene = 0
        for s in range(7):
            scene = scene + (block >= ends[s]).astype(jnp.int32)
        out_ref[block] = scene


def scene_of_block(lengths):
    return pl.pallas_call(
        scene_kernel,
        in_specs=[SMEM],
        out_specs=SMEM,
        out_shape=jax.ShapeDtypeStruct((16,), jnp.int32),
        compiler_params=pltpu.CompilerParams(vmem_limit_bytes=2**20),
        cost_estimate=pl.CostEstimate(flops=20 * 10**9, bytes_accessed=64, transcendentals=0),
    )(lengths)


def in_kernel(x_ref, w_ref, p_ref, o_ref):
    width = 256
    x = x_ref[...]
    total = None
    for n in range(w_ref.shape[1] // width):
        part = slice(n * width, (n + 1) * width)
        z = lax.dot_general(
            w_ref[:, part], x, (((0,), (1,)), ((), ())), preferred_element_type=f32
        )
        term = jnp.dot(p_ref[:, part], gelu(z).astype(bf16), preferred_element_type=f32)
        total = term if total is None else total + term
    half = x.shape[0] // 2
    o_ref[0] = total[:, :half].astype(bf16)
    o_ref[1] = total[:, half:].astype(bf16)


def in_project(x, w, p):
    rows, width = x.shape
    hidden = w.shape[1]
    return pl.pallas_call(
        in_kernel,
        in_specs=[VMEM] * 3,
        out_specs=VMEM,
        out_shape=jax.ShapeDtypeStruct((2, p.shape[0], rows // 2), bf16),
        compiler_params=pltpu.CompilerParams(vmem_limit_bytes=32 * 2**20),
        cost_estimate=pl.CostEstimate(
            flops=2 * rows * hidden * (width + 256),
            bytes_accessed=2 * (rows * width + width * hidden),
            transcendentals=rows * hidden,
        ),
    )(near(x), near(w), near(p))


def feature_kernel(scene_ref, o1_ref, o2_ref, i_ref, keep_ref, sent_ref, acc):
    core = lax.axis_index("c")
    acc[...] = jnp.zeros(acc.shape, f32)
    for turn, o_ref in enumerate((o1_ref, o2_ref)):
        half = core ^ turn
        for k in range(8):
            cols = slice(k * 128, (k + 1) * 128)
            acc[scene_ref[half * 8 + k]] += lax.dot_general(
                o_ref[:, cols],
                i_ref[half, :, cols],
                (((1,), (1,)), ((), ())),
                preferred_element_type=f32,
            )
    for m in range(4):
        pair = jnp.concatenate([acc[m], acc[m + 4]], axis=1)
        for t in range(4):
            even = pair[16 * t : 16 * t + 8, :]
            odd = pair[16 * t + 8 : 16 * t + 16, :]
            keep_ref[t, 8 * m : 8 * m + 8, :] = jnp.where(core == 0, even, odd)
            sent_ref[t, 8 * m : 8 * m + 8, :] = jnp.where(core == 0, odd, even).astype(bf16)


def features(scene, o1, o2, i):
    return pl.pallas_call(
        feature_kernel,
        in_specs=[SMEM, VMEM, VMEM, VMEM],
        out_specs=[VMEM, VMEM],
        out_shape=[jax.ShapeDtypeStruct((4, 32, 128), f32), jax.ShapeDtypeStruct((4, 32, 128), bf16)],
        scratch_shapes=[pltpu.VMEM((8, 64, 64), f32)],
        compiler_params=pltpu.CompilerParams(vmem_limit_bytes=8 * 2**20),
        cost_estimate=pl.CostEstimate(flops=2 * 10**8, bytes_accessed=2**20, transcendentals=0),
    )(scene, near(o1), near(o2), near(i))


def score_kernel(f1_ref, f2_ref, q_ref, out_ref, own, turned, feat):
    group = lax.axis_index("z") * 4 + lax.axis_index("y2") * 2 + lax.axis_index("y1")
    lanes = lax.broadcasted_iota(jnp.int32, (8, 128), 1)
    total = f1_ref[...] + f2_ref[...].astype(f32)
    own[...] = total
    turned[...] = pltpu.roll(total, 64, 1)
    low = lax.broadcasted_iota(jnp.int32, (4, 128), 1) < 64
    for p in range(4):
        even, odd = pl.ds(2 * p, 4, stride=8), pl.ds(2 * p + 1, 4, stride=8)
        cols = slice(128 * p, 128 * p + 128)
        feat[0:4, cols] = jnp.where(low, own[even, :], turned[odd, :])
        feat[4:8, cols] = jnp.where(low, turned[even, :], own[odd, :])
    f = feat[...].astype(bf16)
    for t in range(8):
        rows = []
        for b in range(8):
            bits = dict(z=t & 4, y2=t & 2, y1=t & 1, y0=b & 4, x1=b & 2, x0=b & 1)
            row = 0
            for axis in ORDER:
                row = 2 * row + (bits[axis] > 0)
            rows.append(q_ref[16 * row : 16 * row + 16, :])
        x = lax.dot_general(
            f, jnp.concatenate(rows, axis=0), (((1,), (1,)), ((), ())), preferred_element_type=f32
        )
        other = jnp.where((lanes & 32) == 0, pltpu.roll(x, 96, 1), pltpu.roll(x, 32, 1))
        out_ref[t ^ group] = jnp.where(lax.axis_index("x1") == 1, other, x)


def partial_scores(f1, f2, q):
    return pl.pallas_call(
        score_kernel,
        in_specs=[VMEM] * 3,
        out_specs=VMEM,
        out_shape=jax.ShapeDtypeStruct((8, 8, 128), f32),
        scratch_shapes=[
            pltpu.VMEM((32, 128), f32),
            pltpu.VMEM((32, 128), f32),
            pltpu.VMEM((8, 512), f32),
        ],
        compiler_params=pltpu.CompilerParams(vmem_limit_bytes=8 * 2**20),
        cost_estimate=pl.CostEstimate(flops=2 * 256 * 512 * 1024, bytes_accessed=2**20, transcendentals=0),
    )(near(f1), near(f2), near(q))


def gather(x, axes):
    count = 2 ** len(axes)
    x = lax.all_to_all(jnp.broadcast_to(x[None], (count,) + x.shape), axes, 0, 0)
    return x.reshape((-1,) + x.shape[2:])


NEAR = [(0, 1), (1, 0), (2, 3), (3, 2)]
FAR = [(0, 2), (2, 0), (1, 3), (3, 1)]
tie = lax.optimization_barrier


def local(inputs, up_weight, out_grad, proj_in, proj_out, queries, lengths):
    core = lax.axis_index("c")
    scene, p = tie((scene_of_block(lengths), proj_in.T))
    q = jnp.concatenate([queries, lax.ppermute(queries, "z", SWAP)], axis=0)
    o = lax.dot_general(proj_out, out_grad, (((0,), (1,)), ((), ())), preferred_element_type=f32)
    half = o.shape[1] // 2
    o1 = lax.dynamic_slice_in_dim(o, core * half, half, 1)
    o2 = lax.dynamic_slice_in_dim(o, (1 - core) * half, half, 1)
    o = o1 + lax.ppermute(o2.astype(bf16), "c", SWAP).astype(f32)

    i = in_project(inputs, up_weight, p)

    o, q, i = tie((o, q, i))
    q2 = lax.ppermute(q, "y2", SWAP)
    o2 = lax.ppermute(o.astype(bf16), "zl", NEAR)
    o, o2, q, q2 = tie((o, o2, q, q2))
    q = jnp.concatenate([q, q2], axis=0)
    q = jnp.concatenate([q, lax.ppermute(q, "x1", SWAP)], axis=0)
    q = jnp.concatenate([q, lax.ppermute(q, "y1", SWAP)], axis=0)
    o = o + o2.astype(f32)
    o = o + lax.ppermute(o.astype(bf16), "zl", FAR).astype(f32)
    o1 = o.astype(bf16)
    o2 = lax.ppermute(o1, "c", SWAP)

    f, sent = features(scene, o1, o2, i)
    f = f + lax.ppermute(sent, "c", SWAP).astype(f32)
    q, f = tie((q, f))
    q = gather(q, ("y0", "x0"))
    f = f.reshape((2, 2) + f.shape[1:])
    low, high = lax.axis_index("zl") % 2, lax.axis_index("zl") // 2
    sent = lax.dynamic_index_in_dim(f, 1 - low, 1, False).astype(bf16)
    f = lax.dynamic_index_in_dim(f, low, 1, False) + lax.ppermute(sent, "zl", NEAR).astype(f32)
    sent = lax.dynamic_index_in_dim(f, 1 - high, 0, False).astype(bf16)
    f = lax.dynamic_index_in_dim(f, high, 0, False)
    scores = partial_scores(f, lax.ppermute(sent, "zl", FAR), q)
    return jnp.sum(lax.all_to_all(scores, TENSOR, 0, 0), axis=0)


def solution(mesh):
    fine = Mesh(mesh.devices.reshape(SIZES), PARTS)
    return jax.shard_map(
        local,
        mesh=fine,
        in_specs=(
            P(DP, None),
            P(None, TENSOR),
            P(DP, TENSOR),
            P(TENSOR, None),
            P(TENSOR, None),
            P(DP, TENSOR),
            P(DP, None),
        ),
        out_specs=P(DP, TENSOR),
        check_vma=False,
    )
```

```python
import jax
import jax.numpy as jnp
from jax import lax
from jax.experimental import pallas as pl
from jax.experimental.pallas import tpu as pltpu
from jax.sharding import Mesh
from jax.sharding import PartitionSpec as P

bf16 = jnp.bfloat16
f32 = jnp.float32

PARTS = ("z", "y2", "y1", "y0", "x1", "x0", "zl", "c")
SIZES = (2, 2, 2, 2, 2, 2, 4, 2)
DP = PARTS[:6]
TENSOR = PARTS[6:]
SWAP = [(0, 1), (1, 0)]
ORDER = ("y0", "x0", "x1", "y1", "y2", "z")
VMEM = pl.BlockSpec(memory_space=pltpu.VMEM)
ANY = pl.BlockSpec(memory_space=pl.ANY)
SMEM = pl.BlockSpec(memory_space=pltpu.SMEM)

ERF = (
    7.97884332e-01,
    3.63339859e-02,
    -3.29015638e-05,
    -5.53135740e-05,
    3.98006372e-06,
    -1.34189628e-07,
    1.82394749e-09,
)


def gelu(x):
    u = x * x
    g = ERF[-1]
    for coef in ERF[-2::-1]:
        g = g * u + coef
    half = 0.5 * x
    return half + half * jnp.tanh(x * g)


def near(x):
    return pltpu.with_memory_space_constraint(x, pltpu.VMEM)


def scene_kernel(len_ref, out_ref):
    ends, end = [], 0
    for s in range(8):
        end = end + len_ref[0, s]
        ends.append(end)
    for block in range(16):
        scene = 0
        for s in range(7):
            scene = scene + (block >= ends[s]).astype(jnp.int32)
        out_ref[block] = scene


def scene_of_block(lengths):
    return pl.pallas_call(
        scene_kernel,
        in_specs=[SMEM],
        out_specs=SMEM,
        out_shape=jax.ShapeDtypeStruct((16,), jnp.int32),
        compiler_params=pltpu.CompilerParams(vmem_limit_bytes=2**20),
        cost_estimate=pl.CostEstimate(flops=20 * 10**9, bytes_accessed=64, transcendentals=0),
    )(lengths)


def in_kernel(x_ref, w_ref, p_ref, o_ref):
    width = 256
    x = x_ref[...]
    total = None
    for n in range(w_ref.shape[1] // width):
        part = slice(n * width, (n + 1) * width)
        z = lax.dot_general(
            w_ref[:, part], x, (((0,), (1,)), ((), ())), preferred_element_type=f32
        )
        term = jnp.dot(p_ref[:, part], gelu(z).astype(bf16), preferred_element_type=f32)
        total = term if total is None else total + term
    half = x.shape[0] // 2
    o_ref[0] = total[:, :half].astype(bf16)
    o_ref[1] = total[:, half:].astype(bf16)


def in_project(x, w, p):
    rows, width = x.shape
    hidden = w.shape[1]
    return pl.pallas_call(
        in_kernel,
        in_specs=[VMEM] * 3,
        out_specs=VMEM,
        out_shape=jax.ShapeDtypeStruct((2, p.shape[0], rows // 2), bf16),
        compiler_params=pltpu.CompilerParams(vmem_limit_bytes=32 * 2**20),
        cost_estimate=pl.CostEstimate(
            flops=2 * rows * hidden * (width + 256),
            bytes_accessed=2 * (rows * width + width * hidden),
            transcendentals=rows * hidden,
        ),
    )(near(x), near(w), near(p))


def feature_kernel(scene_ref, o1_ref, o2_ref, i_ref, out_ref, acc):
    core = lax.axis_index("c")
    acc[...] = jnp.zeros(acc.shape, f32)
    for turn, o_ref in enumerate((o1_ref, o2_ref)):
        half = core ^ turn
        for k in range(8):
            cols = slice(k * 128, (k + 1) * 128)
            acc[scene_ref[half * 8 + k]] += lax.dot_general(
                o_ref[:, cols],
                i_ref[half, :, cols],
                (((1,), (1,)), ((), ())),
                preferred_element_type=f32,
            )
    for m in range(4):
        pair = jnp.concatenate([acc[m], acc[m + 4]], axis=1).astype(bf16)
        for t in range(8):
            out_ref[t, 8 * m : 8 * m + 8, :] = pair[8 * t : 8 * t + 8, :]


def features(scene, o1, o2, i):
    return pl.pallas_call(
        feature_kernel,
        in_specs=[SMEM, VMEM, VMEM, VMEM],
        out_specs=VMEM,
        out_shape=jax.ShapeDtypeStruct((8, 32, 128), bf16),
        scratch_shapes=[pltpu.VMEM((8, 64, 64), f32)],
        compiler_params=pltpu.CompilerParams(vmem_limit_bytes=8 * 2**20),
        cost_estimate=pl.CostEstimate(flops=20 * 10**9, bytes_accessed=2**20, transcendentals=0),
    )(scene, near(o1), near(o2), near(i))


def score_kernel(f_ref, q_ref, out_ref, own, turned, feat):
    group = lax.axis_index("z") * 4 + lax.axis_index("y2") * 2
    total = f_ref[0].astype(f32)
    for t in range(1, 8):
        total = total + f_ref[t].astype(f32)
    own[...] = total
    turned[...] = pltpu.roll(total, 64, 1)
    low = lax.broadcasted_iota(jnp.int32, (4, 128), 1) < 64
    for p in range(4):
        even, odd = pl.ds(2 * p, 4, stride=8), pl.ds(2 * p + 1, 4, stride=8)
        cols = slice(128 * p, 128 * p + 128)
        feat[0:4, cols] = jnp.where(low, own[even, :], turned[odd, :])
        feat[4:8, cols] = jnp.where(low, turned[even, :], own[odd, :])
    f = feat[...].astype(bf16)
    for t in range(8):
        rows = []
        for b in range(8):
            bits = dict(z=t & 4, y2=t & 2, y1=t & 1, y0=b & 4, x1=b & 2, x0=b & 1)
            row = 0
            for axis in ORDER:
                row = 2 * row + (bits[axis] > 0)
            rows.append(q_ref[16 * row : 16 * row + 16, :])
        x = lax.dot_general(
            f, jnp.concatenate(rows, axis=0), (((1,), (1,)), ((), ())), preferred_element_type=f32
        )
        out_ref[t ^ group] = x


def partial_scores(f, q):
    return pl.pallas_call(
        score_kernel,
        in_specs=[VMEM] * 2,
        out_specs=VMEM,
        out_shape=jax.ShapeDtypeStruct((8, 8, 128), f32),
        scratch_shapes=[
            pltpu.VMEM((32, 128), f32),
            pltpu.VMEM((32, 128), f32),
            pltpu.VMEM((8, 512), f32),
        ],
        compiler_params=pltpu.CompilerParams(vmem_limit_bytes=8 * 2**20),
        cost_estimate=pl.CostEstimate(flops=2 * 256 * 512 * 1024, bytes_accessed=2**20, transcendentals=0),
    )(f, q)


def gather(x, axes):
    count = 2 ** len(axes)
    x = lax.all_to_all(jnp.broadcast_to(x[None], (count,) + x.shape), axes, 0, 0)
    return x.reshape((-1,) + x.shape[2:])


NEAR = [(0, 1), (1, 0), (2, 3), (3, 2)]
FAR = [(0, 2), (2, 0), (1, 3), (3, 1)]
tie = lax.optimization_barrier


def local(inputs, up_weight, out_grad, proj_in, proj_out, queries, lengths):
    core = lax.axis_index("c")
    scene, p = tie((scene_of_block(lengths), proj_in.T))
    q = jnp.concatenate([queries, lax.ppermute(queries, "z", SWAP)], axis=0)
    o = lax.dot_general(proj_out, out_grad, (((0,), (1,)), ((), ())), preferred_element_type=f32)
    half = o.shape[1] // 2
    o1 = lax.dynamic_slice_in_dim(o, core * half, half, 1)
    o2 = lax.dynamic_slice_in_dim(o, (1 - core) * half, half, 1)
    o = o1 + lax.ppermute(o2.astype(bf16), "c", SWAP).astype(f32)
    i = in_project(inputs, up_weight, p)

    o, q, i = tie((o, q, i))
    o = o + lax.ppermute(o.astype(bf16), "zl", NEAR).astype(f32)
    o = o + lax.ppermute(o.astype(bf16), "zl", FAR).astype(f32)
    o1 = o.astype(bf16)
    o2 = lax.ppermute(o1, "c", SWAP)
    q = jnp.concatenate([q, lax.ppermute(q, "y2", SWAP)], axis=0)
    q = gather(q, ("x1", "y1"))
    q, o1, o2 = tie((q, o1, o2))
    q = gather(q, ("y0", "x0"))
    f = features(scene, o1, o2, i)
    q, f = tie((q, f))
    f = lax.all_to_all(f, TENSOR, 0, 0)
    scores = partial_scores(near(f), near(q))
    return jnp.sum(lax.all_to_all(scores, TENSOR, 0, 0), axis=0)


def solution(mesh):
    fine = Mesh(mesh.devices.reshape(SIZES), PARTS)
    return jax.shard_map(
        local,
        mesh=fine,
        in_specs=(
            P(DP, None),
            P(None, TENSOR),
            P(DP, TENSOR),
            P(TENSOR, None),
            P(TENSOR, None),
            P(DP, TENSOR),
            P(DP, None),
        ),
        out_specs=P(DP, TENSOR),
        check_vma=False,
    )
```

```python
import jax
import jax.numpy as jnp
from jax import lax
from jax.experimental import pallas as pl
from jax.experimental.pallas import tpu as pltpu
from jax.sharding import Mesh
from jax.sharding import PartitionSpec as P

bf16 = jnp.bfloat16
f32 = jnp.float32

PARTS = ("z", "y2", "y1", "y0", "x1", "x0", "zl", "c")
SIZES = (2, 2, 2, 2, 2, 2, 4, 2)
DP = PARTS[:6]
TENSOR = PARTS[6:]
SWAP = [(0, 1), (1, 0)]
ORDER = ("x0", "y0", "x1", "y1", "y2", "z")
VMEM = pl.BlockSpec(memory_space=pltpu.VMEM)
ANY = pl.BlockSpec(memory_space=pl.ANY)
SMEM = pl.BlockSpec(memory_space=pltpu.SMEM)

ERF = (
    7.97884332e-01,
    3.63339859e-02,
    -3.29015638e-05,
    -5.53135740e-05,
    3.98006372e-06,
    -1.34189628e-07,
    1.82394749e-09,
)


def gelu(x):
    u = x * x
    g = ERF[-1]
    for coef in ERF[-2::-1]:
        g = g * u + coef
    half = 0.5 * x
    return half + half * jnp.tanh(x * g)


def near(x):
    return pltpu.with_memory_space_constraint(x, pltpu.VMEM)


def scene_kernel(zero_ref, len_ref, out_ref):
    ends, end = [], 0
    for s in range(8):
        end = end + len_ref[0, s]
        ends.append(end)
    for block in range(16):
        scene = zero_ref[0]
        for s in range(7):
            scene = scene + (block >= ends[s]).astype(jnp.int32)
        out_ref[block] = scene


def scene_of_block(zero, lengths):
    return pl.pallas_call(
        scene_kernel,
        in_specs=[SMEM, SMEM],
        out_specs=SMEM,
        out_shape=jax.ShapeDtypeStruct((16,), jnp.int32),
        compiler_params=pltpu.CompilerParams(vmem_limit_bytes=2**20),
        cost_estimate=pl.CostEstimate(flops=10**6, bytes_accessed=64, transcendentals=0),
    )(zero, lengths)


def mark_kernel(out_ref):
    out_ref[0] = 0


def mark():
    return pl.pallas_call(
        mark_kernel,
        out_specs=SMEM,
        out_shape=jax.ShapeDtypeStruct((1,), jnp.int32),
        compiler_params=pltpu.CompilerParams(vmem_limit_bytes=2**20),
        cost_estimate=pl.CostEstimate(flops=20 * 10**9, bytes_accessed=64, transcendentals=0),
    )()


def in_kernel(x_ref, w_ref, p_ref, o_ref):
    width = 256
    x = x_ref[...]
    total = None
    for n in range(w_ref.shape[1] // width):
        part = slice(n * width, (n + 1) * width)
        z = lax.dot_general(
            w_ref[:, part], x, (((0,), (1,)), ((), ())), preferred_element_type=f32
        )
        term = jnp.dot(p_ref[:, part], gelu(z).astype(bf16), preferred_element_type=f32)
        total = term if total is None else total + term
    half = x.shape[0] // 2
    o_ref[0] = total[:, :half].astype(bf16)
    o_ref[1] = total[:, half:].astype(bf16)


def in_project(x, w, p):
    rows, width = x.shape
    hidden = w.shape[1]
    return pl.pallas_call(
        in_kernel,
        in_specs=[VMEM] * 3,
        out_specs=VMEM,
        out_shape=jax.ShapeDtypeStruct((2, p.shape[0], rows // 2), bf16),
        compiler_params=pltpu.CompilerParams(vmem_limit_bytes=32 * 2**20),
        cost_estimate=pl.CostEstimate(
            flops=2 * rows * hidden * (width + 256),
            bytes_accessed=2 * (rows * width + width * hidden),
            transcendentals=rows * hidden,
        ),
    )(near(x), near(w), near(p))


def feature_kernel(scene_ref, o1_ref, o2_ref, i_ref, out_ref, acc):
    core = lax.axis_index("c")
    acc[...] = jnp.zeros(acc.shape, f32)
    for turn, o_ref in enumerate((o1_ref, o2_ref)):
        half = core ^ turn
        for k in range(8):
            cols = slice(k * 128, (k + 1) * 128)
            acc[scene_ref[half * 8 + k]] += lax.dot_general(
                o_ref[:, cols],
                i_ref[half, :, cols],
                (((1,), (1,)), ((), ())),
                preferred_element_type=f32,
            )
    for m in range(4):
        pair = jnp.concatenate([acc[m], acc[m + 4]], axis=1).astype(bf16)
        for t in range(8):
            out_ref[t, 8 * m : 8 * m + 8, :] = pair[8 * t : 8 * t + 8, :]


def features(scene, o1, o2, i):
    return pl.pallas_call(
        feature_kernel,
        in_specs=[SMEM, VMEM, VMEM, VMEM],
        out_specs=VMEM,
        out_shape=jax.ShapeDtypeStruct((8, 32, 128), bf16),
        scratch_shapes=[pltpu.VMEM((8, 64, 64), f32)],
        compiler_params=pltpu.CompilerParams(vmem_limit_bytes=8 * 2**20),
        cost_estimate=pl.CostEstimate(flops=20 * 10**9, bytes_accessed=2**20, transcendentals=0),
    )(scene, near(o1), near(o2), near(i))


def score_kernel(f_ref, q1_ref, q2_ref, out_ref, own, turned, feat):
    group = lax.axis_index("z") * 4 + lax.axis_index("y2") * 2
    total = f_ref[0].astype(f32)
    for t in range(1, 8):
        total = total + f_ref[t].astype(f32)
    own[...] = total
    turned[...] = pltpu.roll(total, 64, 1)
    low = lax.broadcasted_iota(jnp.int32, (4, 128), 1) < 64
    for p in range(4):
        even, odd = pl.ds(2 * p, 4, stride=8), pl.ds(2 * p + 1, 4, stride=8)
        cols = slice(128 * p, 128 * p + 128)
        feat[0:4, cols] = jnp.where(low, own[even, :], turned[odd, :])
        feat[4:8, cols] = jnp.where(low, turned[even, :], own[odd, :])
    f = feat[...].astype(bf16)
    lanes = lax.broadcasted_iota(jnp.int32, (8, 128), 1)
    for t in range(8):
        rows = []
        for b in range(8):
            bits = dict(z=t & 4, y2=t & 2, y1=t & 1, y0=b & 4, x1=b & 2, x0=b & 1)
            row = 0
            for axis in ORDER:
                row = 2 * row + (bits[axis] > 0)
            ref, row = (q1_ref, row) if row < 32 else (q2_ref, row - 32)
            rows.append(ref[16 * row : 16 * row + 16, :])
        x = lax.dot_general(
            f, jnp.concatenate(rows, axis=0), (((1,), (1,)), ((), ())), preferred_element_type=f32
        )
        for axis, width in (("y0", 64), ("x0", 16)):
            other = jnp.where((lanes & width) == 0, pltpu.roll(x, 128 - width, 1), pltpu.roll(x, width, 1))
            x = jnp.where(lax.axis_index(axis) == 1, other, x)
        out_ref[t ^ group] = x


def partial_scores(f, q1, q2):
    return pl.pallas_call(
        score_kernel,
        in_specs=[VMEM] * 3,
        out_specs=VMEM,
        out_shape=jax.ShapeDtypeStruct((8, 8, 128), f32),
        scratch_shapes=[
            pltpu.VMEM((32, 128), f32),
            pltpu.VMEM((32, 128), f32),
            pltpu.VMEM((8, 512), f32),
        ],
        compiler_params=pltpu.CompilerParams(vmem_limit_bytes=8 * 2**20),
        cost_estimate=pl.CostEstimate(flops=2 * 256 * 512 * 1024, bytes_accessed=2**20, transcendentals=0),
    )(f, q1, q2)


def gather(x, axes):
    count = 2 ** len(axes)
    x = lax.all_to_all(jnp.broadcast_to(x[None], (count,) + x.shape), axes, 0, 0)
    return x.reshape((-1,) + x.shape[2:])


NEAR = [(0, 1), (1, 0), (2, 3), (3, 2)]
FAR = [(0, 2), (2, 0), (1, 3), (3, 1)]
tie = lax.optimization_barrier


def local(inputs, up_weight, out_grad, proj_in, proj_out, queries, lengths):
    core = lax.axis_index("c")
    zero, p = tie((mark(), proj_in.T))
    q = jnp.concatenate([queries, lax.ppermute(queries, "z", SWAP)], axis=0)
    o = lax.dot_general(proj_out, out_grad, (((0,), (1,)), ((), ())), preferred_element_type=f32)
    half = o.shape[1] // 2
    o1 = lax.dynamic_slice_in_dim(o, core * half, half, 1)
    o2 = lax.dynamic_slice_in_dim(o, (1 - core) * half, half, 1)
    o = o1 + lax.ppermute(o2.astype(bf16), "c", SWAP).astype(f32)
    i = in_project(inputs, up_weight, p)

    o, q, i, lengths = tie((o, q, i, lengths))
    scene = scene_of_block(zero, lengths)
    o = o + lax.ppermute(o.astype(bf16), "zl", NEAR).astype(f32)
    o = o + lax.ppermute(o.astype(bf16), "zl", FAR).astype(f32)
    o1 = o.astype(bf16)
    o2 = lax.ppermute(o1, "c", SWAP)
    q = jnp.concatenate([q, lax.ppermute(q, "y2", SWAP)], axis=0)
    q = gather(q, ("x1", "y1"))
    q, o1, o2 = tie((q, o1, o2))
    q = jnp.concatenate([q, lax.ppermute(q, "y0", SWAP)], axis=0)
    f = features(scene, o1, o2, i)
    q, f = tie((q, f))
    q2 = lax.ppermute(q, "x0", SWAP)
    f = lax.all_to_all(f, TENSOR, 0, 0)
    scores = partial_scores(near(f), near(q), near(q2))
    return jnp.sum(lax.all_to_all(scores, TENSOR, 0, 0), axis=0)


def solution(mesh):
    fine = Mesh(mesh.devices.reshape(SIZES), PARTS)
    return jax.shard_map(
        local,
        mesh=fine,
        in_specs=(
            P(DP, None),
            P(None, TENSOR),
            P(DP, TENSOR),
            P(TENSOR, None),
            P(TENSOR, None),
            P(DP, TENSOR),
            P(DP, None),
        ),
        out_specs=P(DP, TENSOR),
        check_vma=False,
    )
```

```python
import jax
import jax.numpy as jnp
from jax import lax
from jax.experimental import pallas as pl
from jax.experimental.pallas import tpu as pltpu
from jax.sharding import Mesh
from jax.sharding import PartitionSpec as P

bf16 = jnp.bfloat16
f32 = jnp.float32

PARTS = ("z", "y2", "y1", "y0", "x1", "x0", "zl", "c")
SIZES = (2, 2, 2, 2, 2, 2, 4, 2)
DP = PARTS[:6]
TENSOR = PARTS[6:]
SWAP = [(0, 1), (1, 0)]
ORDER = ("x0", "y0", "x1", "y1", "y2", "z")
VMEM = pl.BlockSpec(memory_space=pltpu.VMEM)
ANY = pl.BlockSpec(memory_space=pl.ANY)
SMEM = pl.BlockSpec(memory_space=pltpu.SMEM)

ERF = (
    7.97884332e-01,
    3.63339859e-02,
    -3.29015638e-05,
    -5.53135740e-05,
    3.98006372e-06,
    -1.34189628e-07,
    1.82394749e-09,
)


def gelu(x):
    u = x * x
    g = ERF[-1]
    for coef in ERF[-2::-1]:
        g = g * u + coef
    half = 0.5 * x
    return half + half * jnp.tanh(x * g)


def near(x):
    return pltpu.with_memory_space_constraint(x, pltpu.VMEM)


def scene_kernel(zero_ref, len_ref, out_ref):
    ends, end = [], 0
    for s in range(8):
        end = end + len_ref[0, s]
        ends.append(end)
    for block in range(16):
        scene = zero_ref[0]
        for s in range(7):
            scene = scene + (block >= ends[s]).astype(jnp.int32)
        out_ref[block] = scene


def scene_of_block(zero, lengths):
    return pl.pallas_call(
        scene_kernel,
        in_specs=[SMEM, SMEM],
        out_specs=SMEM,
        out_shape=jax.ShapeDtypeStruct((16,), jnp.int32),
        compiler_params=pltpu.CompilerParams(vmem_limit_bytes=2**20),
        cost_estimate=pl.CostEstimate(flops=10**6, bytes_accessed=64, transcendentals=0),
    )(zero, lengths)


def mark_kernel(out_ref):
    out_ref[0] = 0


def mark():
    return pl.pallas_call(
        mark_kernel,
        out_specs=SMEM,
        out_shape=jax.ShapeDtypeStruct((1,), jnp.int32),
        compiler_params=pltpu.CompilerParams(vmem_limit_bytes=2**20),
        cost_estimate=pl.CostEstimate(flops=20 * 10**9, bytes_accessed=64, transcendentals=0),
    )()


def in_kernel(x_ref, w_ref, p_ref, o_ref):
    width = 256
    x = x_ref[...]
    total = None
    for n in range(w_ref.shape[1] // width):
        part = slice(n * width, (n + 1) * width)
        z = lax.dot_general(
            w_ref[:, part], x, (((0,), (1,)), ((), ())), preferred_element_type=f32
        )
        term = jnp.dot(p_ref[:, part], gelu(z).astype(bf16), preferred_element_type=f32)
        total = term if total is None else total + term
    half = x.shape[0] // 2
    o_ref[0] = total[:, :half].astype(bf16)
    o_ref[1] = total[:, half:].astype(bf16)


def in_project(x, w, p):
    rows, width = x.shape
    hidden = w.shape[1]
    return pl.pallas_call(
        in_kernel,
        in_specs=[VMEM] * 3,
        out_specs=VMEM,
        out_shape=jax.ShapeDtypeStruct((2, p.shape[0], rows // 2), bf16),
        compiler_params=pltpu.CompilerParams(vmem_limit_bytes=32 * 2**20),
        cost_estimate=pl.CostEstimate(
            flops=2 * rows * hidden * (width + 256),
            bytes_accessed=2 * (rows * width + width * hidden),
            transcendentals=rows * hidden,
        ),
    )(near(x), near(w), near(p))


def feature_kernel(scene_ref, o1_ref, o2_ref, i_ref, out_ref, acc):
    core = lax.axis_index("c")
    acc[...] = jnp.zeros(acc.shape, f32)
    for turn, o_ref in enumerate((o1_ref, o2_ref)):
        half = core ^ turn
        for k in range(8):
            cols = slice(k * 128, (k + 1) * 128)
            acc[scene_ref[half * 8 + k]] += lax.dot_general(
                o_ref[:, cols],
                i_ref[half, :, cols],
                (((1,), (1,)), ((), ())),
                preferred_element_type=f32,
            )
    for m in range(4):
        pair = jnp.concatenate([acc[m], acc[m + 4]], axis=1).astype(bf16)
        for t in range(8):
            out_ref[t, 8 * m : 8 * m + 8, :] = pair[8 * t : 8 * t + 8, :]


def features(scene, o1, o2, i):
    return pl.pallas_call(
        feature_kernel,
        in_specs=[SMEM, VMEM, VMEM, VMEM],
        out_specs=VMEM,
        out_shape=jax.ShapeDtypeStruct((8, 32, 128), bf16),
        scratch_shapes=[pltpu.VMEM((8, 64, 64), f32)],
        compiler_params=pltpu.CompilerParams(vmem_limit_bytes=8 * 2**20),
        cost_estimate=pl.CostEstimate(flops=20 * 10**9, bytes_accessed=2**20, transcendentals=0),
    )(scene, near(o1), near(o2), near(i))


def score_kernel(f_ref, q1_ref, q2_ref, q3_ref, q4_ref, out_ref, own, turned, feat):
    group = lax.axis_index("z") * 4 + lax.axis_index("y2") * 2
    total = f_ref[0].astype(f32)
    for t in range(1, 8):
        total = total + f_ref[t].astype(f32)
    own[...] = total
    turned[...] = pltpu.roll(total, 64, 1)
    low = lax.broadcasted_iota(jnp.int32, (4, 128), 1) < 64
    for p in range(4):
        even, odd = pl.ds(2 * p, 4, stride=8), pl.ds(2 * p + 1, 4, stride=8)
        cols = slice(128 * p, 128 * p + 128)
        feat[0:4, cols] = jnp.where(low, own[even, :], turned[odd, :])
        feat[4:8, cols] = jnp.where(low, turned[even, :], own[odd, :])
    f = feat[...].astype(bf16)
    lanes = lax.broadcasted_iota(jnp.int32, (8, 128), 1)
    for t in range(8):
        rows = []
        for b in range(8):
            bits = dict(z=t & 4, y2=t & 2, y1=t & 1, y0=b & 4, x1=b & 2, x0=b & 1)
            row = 0
            for axis in ORDER:
                row = 2 * row + (bits[axis] > 0)
            ref, row = (q1_ref, q2_ref, q3_ref, q4_ref)[row // 16], row % 16
            rows.append(ref[16 * row : 16 * row + 16, :])
        x = lax.dot_general(
            f, jnp.concatenate(rows, axis=0), (((1,), (1,)), ((), ())), preferred_element_type=f32
        )
        for axis, width in (("y0", 64), ("x0", 16)):
            other = jnp.where((lanes & width) == 0, pltpu.roll(x, 128 - width, 1), pltpu.roll(x, width, 1))
            x = jnp.where(lax.axis_index(axis) == 1, other, x)
        out_ref[t ^ group] = x


def partial_scores(f, *q):
    return pl.pallas_call(
        score_kernel,
        in_specs=[VMEM] * 5,
        out_specs=VMEM,
        out_shape=jax.ShapeDtypeStruct((8, 8, 128), f32),
        scratch_shapes=[
            pltpu.VMEM((32, 128), f32),
            pltpu.VMEM((32, 128), f32),
            pltpu.VMEM((8, 512), f32),
        ],
        compiler_params=pltpu.CompilerParams(vmem_limit_bytes=8 * 2**20),
        cost_estimate=pl.CostEstimate(flops=2 * 256 * 512 * 1024, bytes_accessed=2**20, transcendentals=0),
    )(f, *q)


def gather(x, axes):
    count = 2 ** len(axes)
    x = lax.all_to_all(jnp.broadcast_to(x[None], (count,) + x.shape), axes, 0, 0)
    return x.reshape((-1,) + x.shape[2:])


NEAR = [(0, 1), (1, 0), (2, 3), (3, 2)]
FAR = [(0, 2), (2, 0), (1, 3), (3, 1)]
tie = lax.optimization_barrier


def local(inputs, up_weight, out_grad, proj_in, proj_out, queries, lengths):
    core = lax.axis_index("c")
    zero, p = tie((mark(), proj_in.T))
    q = jnp.concatenate([queries, lax.ppermute(queries, "z", SWAP)], axis=0)
    o = lax.dot_general(proj_out, out_grad, (((0,), (1,)), ((), ())), preferred_element_type=f32)
    half = o.shape[1] // 2
    o1 = lax.dynamic_slice_in_dim(o, core * half, half, 1)
    o2 = lax.dynamic_slice_in_dim(o, (1 - core) * half, half, 1)
    o = o1 + lax.ppermute(o2.astype(bf16), "c", SWAP).astype(f32)
    i = in_project(inputs, up_weight, p)

    o, q, i, lengths = tie((o, q, i, lengths))
    scene = scene_of_block(zero, lengths)
    o = o + lax.ppermute(o.astype(bf16), "zl", NEAR).astype(f32)
    o = o + lax.ppermute(o.astype(bf16), "zl", FAR).astype(f32)
    o1 = o.astype(bf16)
    o2 = lax.ppermute(o1, "c", SWAP)
    q = jnp.concatenate([q, lax.ppermute(q, "y2", SWAP)], axis=0)
    q = gather(q, ("x1", "y1"))
    q, o1, o2 = tie((q, o1, o2))
    q_y = lax.ppermute(q, "y0", SWAP)
    q_x = lax.ppermute(q, "x0", SWAP)
    f = features(scene, o1, o2, i)
    q_y, q_x, f = tie((q_y, q_x, f))
    q_xy = lax.ppermute(q_y, "x0", SWAP)
    f = lax.all_to_all(f, TENSOR, 0, 0)
    scores = partial_scores(near(f), near(q), near(q_y), near(q_x), near(q_xy))
    return jnp.sum(lax.all_to_all(scores, TENSOR, 0, 0), axis=0)


def solution(mesh):
    fine = Mesh(mesh.devices.reshape(SIZES), PARTS)
    return jax.shard_map(
        local,
        mesh=fine,
        in_specs=(
            P(DP, None),
            P(None, TENSOR),
            P(DP, TENSOR),
            P(TENSOR, None),
            P(TENSOR, None),
            P(DP, TENSOR),
            P(DP, None),
        ),
        out_specs=P(DP, TENSOR),
        check_vma=False,
    )
```
